512 devices in a mesh: frame: 64 (over z, y_lo, core), head: 8 (over x, y_hi).
Axes of the slice: x: 4, y: 4 (y_hi: 2, y_lo: 2; y = y_hi * 2 + y_lo), z: 16, core: 2. Of those that a mesh axis runs over, the one named last changes fastest.
Arguments:
- queries: bfloat16 [64, 512, 5120], P('frame', 'head'), may hold values from -80 to 80
- keys: bfloat16 [64, 512, 5120], P('frame', 'head'), may hold values from -80 to 80
- values: bfloat16 [64, 512, 5120], P('frame', 'head'), may hold values from -6 to 6
- residual: bfloat16 [64, 512, 5120], P('frame', 'head'), may hold values from -4 to 4
- q_gain: float32 [5120], replicated, may hold values from 1 to 3
- k_gain: float32 [5120], replicated, may hold values from 1 to 3
- gate_table: float32 [128, 5120], P(None, 'head'), may hold values from 0.5 to 3
- levels: int32 [64], P('frame'), may hold values from 0 to 127, as said below
- offsets: int32 [64], P('frame'), may hold values from 0 to 2, as said below
- incoming: bfloat16 [512, 5120], P('head'), may hold values from -6 to 6
Outputs:
- queue_next: bfloat16 [64, 512, 5120], P('frame', 'head')
The draws below stay inside these ranges and needn't reach their ends.
Inputs may be any that keep to these rules, and one draw needn't show every extreme that they name: levels rise strictly along the queue; levels[f] is 2 f or 2 f + 1, with levels[0] = 0 and the last frame at 127. offsets[f] = (f + s) mod 3 for one shift s of 0 to 2: the windows are runs of 3 consecutive frames starting at frame -s.
All inputs are finite; a program needn't handle non-finite values.
Results may differ from the reference program's by a relative error of at most 0.0098.
Values may be sent and summed in bfloat16 or wider, within the bound.
No kernel may reach another device: no remote copies, remote signals or barrier semaphores. Data moves between devices by JAX's collectives and lax.ppermute only.
A program may use at most 64 MiB of HBM per device.

```python
import math
import jax
import jax.numpy as jnp
from jax import lax

D = 5120
HEADS = 40
HD = 128
TOKF = 512
W = 3
FRAMES = 64
LEVELS = 128


def projected(key, own):
    drawn = jnp.clip(jax.random.normal(jax.random.fold_in(key, own), (FRAMES, TOKF, D), jnp.float32), -6.0, 6.0)
    return drawn.astype(jnp.bfloat16)


def draw_queries(key, part):
    return projected(key, 3)


def draw_keys(key, part):
    return projected(key, 4)


def draw_levels(key, part):
    key = jax.random.fold_in(key, 5)
    extra = jax.random.randint(key, (FRAMES,), 0, 2)
    extra = extra.at[0].set(0).at[FRAMES - 1].set(1)
    return (2 * jnp.arange(FRAMES, dtype=jnp.int32) + extra).astype(jnp.int32)


def draw_offsets(key, part):
    key = jax.random.fold_in(key, 6)
    start = jax.random.randint(key, (), 0, W)
    return ((jnp.arange(FRAMES, dtype=jnp.int32) + start) % W).astype(jnp.int32)


def block_levels(own_key, extent, pieces, smallest, top_value):
    factor_of, own = 1.0, jax.random.fold_in(own_key, 6)
    for position, shards_of in pieces:
        draws = jnp.exp(jax.random.uniform(jax.random.fold_in(own, position), (shards_of,), jnp.float32, smallest / len(pieces), top_value / len(pieces)))
        factor_of = factor_of * jnp.repeat(draws, extent[position] // shards_of).reshape([-1 if axis == position else 1 for axis in range(len(extent))])
    return factor_of


def centred(own_key, extent, width, limit, shards=(), kind=jnp.bfloat16):
    drawn = width * jax.random.normal(own_key, extent, jnp.float32)
    if shards:
        drawn = drawn * block_levels(own_key, extent, shards, -0.22, 0.18)
    return jnp.clip(drawn, -limit, limit).astype(kind)


def setup_inputs(seed: int = 0) -> dict:
    key_list = jax.random.split(jax.random.key(seed), 11)
    return {
        "queries": draw_queries(jax.random.fold_in(key_list[10], 71), 0),
        "keys": draw_keys(jax.random.fold_in(key_list[10], 71), 0),
        "values": centred(key_list[2], (FRAMES, TOKF, D), 1.0, 6.0, ((0, 64), (1, 8))),
        "residual": centred(key_list[3], (FRAMES, TOKF, D), 0.5, 4.0, ((0, 64), (1, 8))),
        "q_gain": jnp.clip(jnp.exp(jax.random.uniform(key_list[4], (D,), jnp.float32, math.log(1.0), math.log(3.0))), 1.0, 3.0),
        "k_gain": jnp.clip(jnp.exp(jax.random.uniform(key_list[5], (D,), jnp.float32, math.log(1.0), math.log(3.0))), 1.0, 3.0),
        "gate_table": jnp.clip(0.5 + 2.5 * jax.random.uniform(key_list[6], (LEVELS, D), jnp.float32) ** block_levels(key_list[6], (LEVELS, D), ((1, 8),), -0.2, 0.2), 0.5, 3.0),
        "levels": draw_levels(jax.random.fold_in(key_list[10], 71), 0),
        "offsets": draw_offsets(jax.random.fold_in(key_list[10], 71), 0),
        "incoming": centred(key_list[9], (TOKF, D), 1.0, 6.0, ((0, 8),)),
    }


def normed(values_in, gain):
    wide = values_in.astype(jnp.float32)
    power = lax.optimization_barrier(jnp.mean(wide * wide, axis=-1, keepdims=True))
    return (wide * lax.rsqrt(power + 1e-06) * gain).astype(jnp.bfloat16)

def reference(queries, keys, values, residual, q_gain, k_gain, gate_table, levels, offsets, incoming):
    reach = W - 1
    span = 2 * reach + 1
    query_normed = normed(queries, q_gain).reshape(FRAMES, TOKF, HEADS, HD)
    key_normed = normed(keys, k_gain).reshape(FRAMES, TOKF, HEADS, HD)
    value_heads = values.reshape(FRAMES, TOKF, HEADS, HD)
    key_padded = jnp.pad(key_normed, ((reach, reach), (0, 0), (0, 0), (0, 0)))
    value_padded = jnp.pad(value_heads, ((reach, reach), (0, 0), (0, 0), (0, 0)))

    def one_frame(packed):
        query_frame, offset, level, frame_id = packed
        key_window = lax.dynamic_slice_in_dim(key_padded, frame_id, span, 0).reshape(span * TOKF, HEADS, HD)
        value_window = lax.dynamic_slice_in_dim(value_padded, frame_id, span, 0).reshape(span * TOKF, HEADS, HD)
        distance = jnp.arange(span, dtype=jnp.int32) - reach
        target = frame_id + distance
        allowed = (distance >= -offset) & (distance <= W - 1 - offset) & (target >= 0) & (target < FRAMES)
        allowed = jnp.repeat(allowed, TOKF)
        scores = jnp.einsum('thc,khc->htk', query_frame.astype(jnp.float32), key_window.astype(jnp.float32)) / jnp.sqrt(jnp.float32(HD))
        scores = jnp.where(allowed[None, None, :], scores, jnp.float32(-1e+30))
        top = lax.optimization_barrier(jnp.max(scores, axis=-1, keepdims=True))
        weights = jnp.exp(scores - top)
        total = lax.optimization_barrier(jnp.sum(weights, axis=-1))
        rounded = lax.optimization_barrier(weights.astype(jnp.bfloat16))
        numer = jnp.einsum('htk,khc->thc', rounded.astype(jnp.float32), value_window.astype(jnp.float32))
        ratio = numer / jnp.transpose(total)[:, :, None]
        gate = gate_table[level]
        return (ratio.reshape(TOKF, D) * gate[None, :]).astype(jnp.bfloat16)
    frame_ids = jnp.arange(FRAMES, dtype=jnp.int32)
    attended = lax.map(one_frame, (query_normed, offsets, levels, frame_ids))
    updated = (residual.astype(jnp.float32) + attended.astype(jnp.float32)).astype(jnp.bfloat16)
    return jnp.concatenate([incoming[None], updated[:-1]], axis=0)
```

```python
import functools
import math
import jax
import jax.numpy as jnp
from jax import lax
from jax.experimental import pallas as pl
from jax.experimental.pallas import tpu as pltpu
from jax.sharding import Mesh, PartitionSpec as P

HD = 128
W = 3
REACH = W - 1
SLOTS = 4
GROUPS = 8
OWN = 5
ROWS = 64
PART = ROWS // SLOTS
KV_ROWS = 2 * (ROWS + PART)
Q_ROWS = 2 * ROWS + 16
O_ROWS = 2 * ROWS + 16
LOG2E = math.log2(math.e)
SCALE = LOG2E / math.sqrt(HD)
FAR = 1e30
VMEM = pltpu.VMEM


def params():
    return pltpu.CompilerParams(vmem_limit_bytes=48 * 1024 * 1024)


def lanes(head):
    return slice(head * HD, (head + 1) * HD)


def scale_of(wide):
    return lax.rsqrt(jnp.mean(wide * wide, axis=-1, keepdims=True) + 1e-06)


def pack_kv_kernel(keys, values, gain, out):
    by = scale_of(keys[...].astype(jnp.float32))
    for group in range(GROUPS):
        for own in range(OWN):
            at = lanes(group * OWN + own)
            key = (keys[:, at].astype(jnp.float32) * by * gain[:, at]).astype(jnp.bfloat16)
            value = values[:, at]
            if own < SLOTS:
                out[own * GROUPS + group, 0:ROWS, :] = key
                out[own * GROUPS + group, ROWS + PART : 2 * ROWS + PART, :] = value
            else:
                for slot in range(SLOTS):
                    part = slice(slot * PART, (slot + 1) * PART)
                    out[slot * GROUPS + group, ROWS : ROWS + PART, :] = key[part]
                    out[slot * GROUPS + group, 2 * ROWS + PART : KV_ROWS, :] = value[part]


def pack_q_kernel(levels, queries, gain, out):
    by = scale_of(queries[...].astype(jnp.float32))
    level = jnp.full((16, HD), levels[0], jnp.int32).astype(jnp.float32).astype(jnp.bfloat16)
    for group in range(GROUPS):
        for own in range(OWN):
            at = lanes(group * OWN + own)
            query = (queries[:, at].astype(jnp.float32) * by * gain[:, at]).astype(jnp.bfloat16)
            if own < SLOTS:
                out[own * GROUPS + group, 0:ROWS, :] = query
                out[own * GROUPS + group, 2 * ROWS : Q_ROWS, :] = level
            else:
                for slot in range(SLOTS):
                    out[slot * GROUPS + group, ROWS : 2 * ROWS, :] = query


def attend_kernel(
    frames, first_out, planes, tile, offsets, left, mine, right, queries, gates, out, key_all, value_all, key_part, value_part
):
    plane = lax.axis_index("plane")
    slot = lax.axis_index("slot")
    count = planes * SLOTS
    phase = lax.rem(offsets[0] + W * count - (plane * SLOTS + slot), W)
    blocks = 2 * REACH + SLOTS
    ones = jnp.ones((ROWS * GROUPS, HD), jnp.bfloat16)
    for j in range(min(frames), max(frames) + 2 * REACH + 1):
        if j < REACH:
            ref, base = left, j * GROUPS
        elif j < REACH + SLOTS:
            ref, base = mine, (j - REACH) * GROUPS
        else:
            ref, base = right, (j - REACH - SLOTS) * GROUPS
        from_all = slice(base, base + GROUPS)
        key_all[j] = ref[from_all, 0:ROWS, :].reshape(ROWS * GROUPS, HD)
        key_part[j] = ref[from_all, ROWS : ROWS + PART, :].reshape(PART * GROUPS, HD)
        value_all[j, :, 0:HD] = ref[from_all, ROWS + PART : 2 * ROWS + PART, :].reshape(ROWS * GROUPS, HD)
        value_all[j, :, HD:] = ones
        value_part[j, :, 0:HD] = ref[from_all, 2 * ROWS + PART : KV_ROWS, :].reshape(PART * GROUPS, HD)
        value_part[j, :, HD:] = ones[: PART * GROUPS]

    def softmaxed(query, key_ref, value_ref, start, allowed):
        scores = [
            lax.dot_general(
                query, key_ref[start + b], (((1,), (1,)), ((), ())), preferred_element_type=jnp.float32
            )
            for b in range(W)
        ]
        tops = [
            jnp.where(allowed[b], jnp.max(scores[b], axis=-1, keepdims=True), -FAR) for b in range(W)
        ]
        top = functools.reduce(jnp.maximum, tops)
        total = None
        for b in range(W):
            weights = jnp.exp2((scores[b] - jnp.where(allowed[b], top, FAR)) * SCALE)
            term = jnp.dot(
                weights.astype(jnp.bfloat16), value_ref[start + b], preferred_element_type=jnp.float32
            )
            total = term if total is None else total + term
        return top, total[:, :HD], total[:, HD:]

    row = lax.broadcasted_iota(jnp.int32, (16, HD), 0)
    level_row = lax.broadcasted_iota(jnp.int32, (gates.shape[0], HD), 0).astype(jnp.float32)
    spot = lax.broadcasted_iota(jnp.int32, (ROWS * GROUPS, HD), 0) % ROWS == lax.broadcasted_iota(
        jnp.int32, (ROWS * GROUPS, HD), 1
    )
    blocks_of = tile // ROWS
    for i in frames:
        frame = plane * SLOTS + i
        offset = lax.rem(frame + phase, W)
        start = i + REACH - offset
        allowed = [
            (frame - offset + b >= 0) & (frame - offset + b < count) for b in range(W)
        ]
        level = queries[i * GROUPS, 2 * ROWS : 2 * ROWS + 1, :].astype(jnp.float32)
        picked = level_row == level

        def gate_of(at):
            return jnp.sum(jnp.where(picked, gates[:, at], 0.0), axis=0, keepdims=True)

        gate = gate_of(pl.ds(pl.multiple_of(slot * HD, HD), HD))
        gate_shared = gate_of(pl.ds(SLOTS * HD, HD))
        to = (i - frames[0] + first_out) * GROUPS

        def step(n, carry):
            query = queries[pl.ds(i * GROUPS + n * blocks_of, blocks_of), 0:ROWS, :].reshape(tile, HD)
            _, numer, total = softmaxed(query, key_all, value_all, start, allowed)
            done = (numer / total * gate).astype(jnp.bfloat16).reshape(blocks_of, ROWS, HD)
            out[pl.ds(to + n * blocks_of, blocks_of), 0:ROWS, :] = done
            return carry

        lax.fori_loop(0, ROWS * GROUPS // tile, step, 0)

        query = queries[i * GROUPS : (i + 1) * GROUPS, ROWS : 2 * ROWS, :].reshape(ROWS * GROUPS, HD)
        top, numer, total = softmaxed(query, key_part, value_part, start, allowed)
        done = (numer / total * gate_shared).astype(jnp.bfloat16).reshape(GROUPS, ROWS, HD)
        out[to : to + GROUPS, ROWS : 2 * ROWS, :] = done
        weight = top * SCALE + jnp.log(total) * LOG2E
        weight = jnp.where(spot, weight, 0.0).reshape(GROUPS, ROWS, HD).sum(axis=1)
        high = weight.astype(jnp.bfloat16).astype(jnp.float32)
        rest = weight - high
        middle = rest.astype(jnp.bfloat16).astype(jnp.float32)
        low = rest - middle
        for t in range(GROUPS):
            at = slice(t, t + 1)
            three = jnp.where(row == 0, high[at], jnp.where(row == 1, middle[at], low[at]))
            out[to + t, 2 * ROWS : O_ROWS, :] = three.astype(jnp.bfloat16)


def combine_kernel(parts, residual, incoming, out):
    first = (lax.axis_index("plane") == 0) & (lax.axis_index("slot") == 0)

    @pl.when(first)
    def _():
        out[...] = incoming[...]

    @pl.when(jnp.logical_not(first))
    def _():
        sent = parts[:, 2 * ROWS : O_ROWS, :].astype(jnp.float32)
        row = lax.broadcasted_iota(jnp.int32, sent.shape, 1)
        weight = jnp.sum(jnp.where(row < 3, sent, 0.0), axis=1).reshape(SLOTS, GROUPS, HD)
        weight = jnp.exp2(weight - jnp.max(weight, axis=0, keepdims=True))
        weight = weight / jnp.sum(weight, axis=0, keepdims=True)
        weight = weight.reshape(SLOTS * GROUPS, HD)
        weight = jnp.concatenate([weight, jnp.zeros((HD - SLOTS * GROUPS, HD), jnp.float32)])
        weight = weight.T[:ROWS]
        for group in range(GROUPS):
            shared = None
            for slot in range(SLOTS):
                r = slot * GROUPS + group
                at = lanes(group * OWN + slot)
                updated = residual[:, at].astype(jnp.float32) + parts[r, 0:ROWS, :].astype(jnp.float32)
                out[:, at] = updated.astype(jnp.bfloat16)
                term = weight[:, r : r + 1] * parts[r, ROWS : 2 * ROWS, :].astype(jnp.float32)
                shared = term if shared is None else shared + term
            at = lanes(group * OWN + SLOTS)
            shared = shared.astype(jnp.bfloat16).astype(jnp.float32)
            out[:, at] = (residual[:, at].astype(jnp.float32) + shared).astype(jnp.bfloat16)


def whole(count):
    return [pl.BlockSpec(memory_space=VMEM)] * count


def on_device(
    planes, queries, keys, values, residual, q_gain, k_gain, gate_table, levels, offsets, incoming
):
    smem = pl.BlockSpec(memory_space=pltpu.SMEM)
    dests = SLOTS * GROUPS
    exchange = lambda x: lax.all_to_all(x, ("slot", "group"), 0, 0, tiled=True)
    up = [(z, (z + 1) % planes) for z in range(planes)]
    down = [(z, (z - 1) % planes) for z in range(planes)]
    count = planes * SLOTS

    kv = pl.pallas_call(
        pack_kv_kernel,
        out_shape=jax.ShapeDtypeStruct((dests, KV_ROWS, HD), jnp.bfloat16),
        in_specs=whole(3),
        out_specs=whole(1)[0],
        compiler_params=params(),
        name="pack_kv",
    )(keys[0], values[0], k_gain[None])
    kv = exchange(kv)
    packed = pl.pallas_call(
        pack_q_kernel,
        out_shape=jax.ShapeDtypeStruct((dests, Q_ROWS, HD), jnp.bfloat16),
        in_specs=[smem] + whole(2),
        out_specs=whole(1)[0],
        compiler_params=params(),
        name="pack_q",
    )(levels, queries[0], q_gain[None])
    query = exchange(packed)
    edge = REACH * GROUPS
    right = lax.ppermute(kv[:edge], "plane", down)
    left = lax.ppermute(kv[dests - edge :], "plane", up)
    moved = lax.ppermute(residual[0], ("plane", "slot"), [(f, (f + 1) % count) for f in range(count)])

    def attend(frames, first_out, slots_out, name):
        blocks = 2 * REACH + SLOTS
        units = len(frames)
        return pl.pallas_call(
            functools.partial(attend_kernel, frames, first_out, planes, 256),
            out_shape=jax.ShapeDtypeStruct((slots_out * GROUPS, O_ROWS, HD), jnp.bfloat16),
            in_specs=[smem] + whole(5),
            out_specs=whole(1)[0],
            scratch_shapes=[
                VMEM((blocks, ROWS * GROUPS, HD), jnp.bfloat16),
                VMEM((blocks, ROWS * GROUPS, 2 * HD), jnp.bfloat16),
                VMEM((blocks, PART * GROUPS, HD), jnp.bfloat16),
                VMEM((blocks, PART * GROUPS, 2 * HD), jnp.bfloat16),
            ],
            compiler_params=params(),
            cost_estimate=pl.CostEstimate(
                flops=units * 500_000_000, bytes_accessed=4_000_000, transcendentals=units * 1_000_000
            ),
            name=name,
        )(offsets, left, kv, right, query, gate_table)

    last = lax.ppermute(attend((SLOTS - 1,), 0, 1, "attend_last"), "plane", up)
    others = attend(tuple(range(SLOTS - 1)), 1, SLOTS, "attend_others")
    parts = exchange(lax.dynamic_update_slice(others, last, (0, 0, 0)))
    updated = pl.pallas_call(
        combine_kernel,
        out_shape=jax.ShapeDtypeStruct(incoming.shape, jnp.bfloat16),
        in_specs=whole(3),
        out_specs=whole(1)[0],
        compiler_params=params(),
        name="combine",
    )(parts, moved, incoming)
    return updated[None]


def solution(mesh):
    planes = mesh.shape["frame"] // SLOTS
    inner = Mesh(
        mesh.devices.reshape(planes, SLOTS, GROUPS), ("plane", "slot", "group")
    )
    frame = ("plane", "slot")
    tokens = P(frame, "group", None)
    placed = (
        tokens,
        tokens,
        tokens,
        tokens,
        P(),
        P(),
        P(None, "group"),
        P(frame),
        P(frame),
        P("group", None),
    )
    return jax.shard_map(
        functools.partial(on_device, planes), mesh=inner, in_specs=placed, out_specs=tokens, check_vma=False
    )
```

```python
import functools
import math
import jax
import jax.numpy as jnp
from jax import lax
from jax.experimental import pallas as pl
from jax.experimental.pallas import tpu as pltpu
from jax.sharding import Mesh, PartitionSpec as P

HD = 128
W = 3
REACH = W - 1
SLOTS = 4
GROUPS = 8
OWN = 5
ROWS = 64
PART = ROWS // SLOTS
CHUNK = 16
KV_ROWS = 2 * (ROWS + PART)
Q_ROWS = 2 * ROWS + 16
O_ROWS = 2 * ROWS + 16
SCALE = 1.0 / math.sqrt(HD)
FAR = 1e30
VMEM = pltpu.VMEM
HBM = pl.BlockSpec(memory_space=pltpu.HBM)


def params(mib=48):
    return pltpu.CompilerParams(vmem_limit_bytes=mib * 1024 * 1024)


def lanes(head):
    return slice(head * HD, (head + 1) * HD)


def scale_of(wide):
    return lax.rsqrt(jnp.mean(wide * wide, axis=-1, keepdims=True) + 1e-06)


def pack_kv_kernel(keys_in, values_in, gain, out, keys, values, blocks, in_sems, out_sems):
    chunks = ROWS // CHUNK
    reads = []
    for n, (source, target) in enumerate(((keys_in, keys), (values_in, values))):
        for c in range(chunks):
            at = pl.ds(c * CHUNK, CHUNK)
            read = pltpu.make_async_copy(source.at[at], target.at[at], in_sems.at[n * chunks + c])
            read.start()
            reads.append(read)
    scales = []
    for c in range(chunks):
        reads[c].wait()
        scales.append(scale_of(keys[c * CHUNK : (c + 1) * CHUNK, :].astype(jnp.float32)))
    by = jnp.concatenate(scales)
    for read in reads[chunks:]:
        read.wait()

    def pair(head):
        at = lanes(head)
        key = (keys[:, at].astype(jnp.float32) * by * gain[:, at]).astype(jnp.bfloat16)
        return key, values[:, at]

    for group in range(GROUPS):
        key, value = pair(group * OWN + SLOTS)
        for slot in range(SLOTS):
            part = slice(slot * PART, (slot + 1) * PART)
            blocks[slot * GROUPS + group, ROWS : ROWS + PART, :] = key[part]
            blocks[slot * GROUPS + group, 2 * ROWS + PART : KV_ROWS, :] = value[part]
    writes = []
    for slot in range(SLOTS):
        for group in range(GROUPS):
            key, value = pair(group * OWN + slot)
            blocks[slot * GROUPS + group, 0:ROWS, :] = key
            blocks[slot * GROUPS + group, ROWS + PART : 2 * ROWS + PART, :] = value
        at = pl.ds(slot * GROUPS, GROUPS)
        write = pltpu.make_async_copy(blocks.at[at], out.at[at], out_sems.at[slot])
        write.start()
        writes.append(write)
    for write in writes:
        write.wait()


def pack_q_kernel(levels, queries, gain, out):
    by = scale_of(queries[...].astype(jnp.float32))
    level = jnp.full((16, HD), levels[0], jnp.int32).astype(jnp.float32).astype(jnp.bfloat16)
    for group in range(GROUPS):
        for own in range(OWN):
            at = lanes(group * OWN + own)
            query = (queries[:, at].astype(jnp.float32) * by * gain[:, at]).astype(jnp.bfloat16)
            if own < SLOTS:
                out[own * GROUPS + group, 0:ROWS, :] = query
                out[own * GROUPS + group, 2 * ROWS : Q_ROWS, :] = level
            else:
                for slot in range(SLOTS):
                    out[slot * GROUPS + group, ROWS : 2 * ROWS, :] = query


def attend_kernel(
    frames, first_out, planes, tile, offsets, left, mine, right, queries, gates, out_ref, key_all, value_all, key_part, value_part, out, sems
):
    plane = lax.axis_index("plane")
    slot = lax.axis_index("slot")
    count = planes * SLOTS
    phase = lax.rem(offsets[0] + W * count - (plane * SLOTS + slot), W)
    blocks = 2 * REACH + SLOTS
    ones = jnp.ones((ROWS * GROUPS, HD), jnp.bfloat16)
    for j in range(min(frames), max(frames) + 2 * REACH + 1):
        if j < REACH:
            ref, base = left, j * GROUPS
        elif j < REACH + SLOTS:
            ref, base = mine, (j - REACH) * GROUPS
        else:
            ref, base = right, (j - REACH - SLOTS) * GROUPS
        from_all = slice(base, base + GROUPS)
        key_all[j] = ref[from_all, 0:ROWS, :].reshape(ROWS * GROUPS, HD)
        key_part[j] = ref[from_all, ROWS : ROWS + PART, :].reshape(PART * GROUPS, HD)
        value_all[j, :, 0:HD] = ref[from_all, ROWS + PART : 2 * ROWS + PART, :].reshape(ROWS * GROUPS, HD)
        value_all[j, :, HD:] = ones
        value_part[j, :, 0:HD] = ref[from_all, 2 * ROWS + PART : KV_ROWS, :].reshape(PART * GROUPS, HD)
        value_part[j, :, HD:] = ones[: PART * GROUPS]

    def softmaxed(query, key_ref, value_ref, start, allowed):
        scores = [
            lax.dot_general(
                query, key_ref[start + b], (((1,), (1,)), ((), ())), preferred_element_type=jnp.float32
            )
            for b in range(W)
        ]
        tops = [
            jnp.where(
                allowed[b],
                functools.reduce(
                    jnp.maximum, [scores[b][:, lanes(n)] for n in range(scores[b].shape[1] // HD)]
                ),
                -FAR,
            )
            for b in range(W)
        ]
        top = jnp.max(functools.reduce(jnp.maximum, tops), axis=-1, keepdims=True)
        total = None
        for b in range(W):
            weights = jnp.exp((scores[b] - jnp.where(allowed[b], top, FAR)) * SCALE)
            term = jnp.dot(
                weights.astype(jnp.bfloat16), value_ref[start + b], preferred_element_type=jnp.float32
            )
            total = term if total is None else total + term
        return top, total[:, :HD], total[:, HD:]

    row = lax.broadcasted_iota(jnp.int32, (16, HD), 0)
    level_row = lax.broadcasted_iota(jnp.int32, (gates.shape[0], HD), 0).astype(jnp.float32)
    spot = lax.broadcasted_iota(jnp.int32, (ROWS * GROUPS, HD), 0) % ROWS == lax.broadcasted_iota(
        jnp.int32, (ROWS * GROUPS, HD), 1
    )
    blocks_of = tile // ROWS
    writes = []
    for i in frames:
        frame = plane * SLOTS + i
        offset = lax.rem(frame + phase, W)
        start = i + REACH - offset
        allowed = [
            (frame - offset + b >= 0) & (frame - offset + b < count) for b in range(W)
        ]
        level = queries[i * GROUPS, 2 * ROWS : 2 * ROWS + 1, :].astype(jnp.float32)
        picked = level_row == level

        def gate_of(at):
            return jnp.sum(jnp.where(picked, gates[:, at], 0.0), axis=0, keepdims=True)

        gate = gate_of(pl.ds(pl.multiple_of(slot * HD, HD), HD))
        gate_shared = gate_of(pl.ds(SLOTS * HD, HD))
        to = (i - frames[0]) * GROUPS

        for n in range(ROWS * GROUPS // tile):
            first = i * GROUPS + n * blocks_of
            query = queries[first : first + blocks_of, 0:ROWS, :].reshape(tile, HD)
            _, numer, total = softmaxed(query, key_all, value_all, start, allowed)
            done = (numer / total * gate).astype(jnp.bfloat16).reshape(blocks_of, ROWS, HD)
            first = to + n * blocks_of
            out[first : first + blocks_of, 0:ROWS, :] = done

        query = queries[i * GROUPS : (i + 1) * GROUPS, ROWS : 2 * ROWS, :].reshape(ROWS * GROUPS, HD)
        top, numer, total = softmaxed(query, key_part, value_part, start, allowed)
        done = (numer / total * gate_shared).astype(jnp.bfloat16).reshape(GROUPS, ROWS, HD)
        out[to : to + GROUPS, ROWS : 2 * ROWS, :] = done
        weight = top * SCALE + jnp.log(total)
        weight = jnp.where(spot, weight, 0.0).reshape(GROUPS, ROWS, HD).sum(axis=1)
        high = weight.astype(jnp.bfloat16).astype(jnp.float32)
        rest = weight - high
        middle = rest.astype(jnp.bfloat16).astype(jnp.float32)
        low = rest - middle
        for t in range(GROUPS):
            at = slice(t, t + 1)
            three = jnp.where(row == 0, high[at], jnp.where(row == 1, middle[at], low[at]))
            out[to + t, 2 * ROWS : O_ROWS, :] = three.astype(jnp.bfloat16)
        write = pltpu.make_async_copy(
            out.at[pl.ds(to, GROUPS)],
            out_ref.at[pl.ds(to + first_out * GROUPS, GROUPS)],
            sems.at[i - frames[0]],
        )
        write.start()
        writes.append(write)
    for write in writes:
        write.wait()


def combine_kernel(parts, residual, incoming, out):
    first = (lax.axis_index("plane") == 0) & (lax.axis_index("slot") == 0)

    @pl.when(first)
    def _():
        out[...] = incoming[...]

    @pl.when(jnp.logical_not(first))
    def _():
        sent = parts[:, 2 * ROWS : O_ROWS, :].astype(jnp.float32)
        row = lax.broadcasted_iota(jnp.int32, sent.shape, 1)
        weight = jnp.sum(jnp.where(row < 3, sent, 0.0), axis=1).reshape(SLOTS, GROUPS, HD)
        weight = jnp.exp(weight - jnp.max(weight, axis=0, keepdims=True))
        weight = weight / jnp.sum(weight, axis=0, keepdims=True)
        weight = weight.reshape(SLOTS * GROUPS, HD)
        weight = jnp.concatenate([weight, jnp.zeros((HD - SLOTS * GROUPS, HD), jnp.float32)])
        weight = weight.T[:ROWS]
        for group in range(GROUPS):
            shared = None
            for slot in range(SLOTS):
                r = slot * GROUPS + group
                at = lanes(group * OWN + slot)
                updated = residual[:, at].astype(jnp.float32) + parts[r, 0:ROWS, :].astype(jnp.float32)
                out[:, at] = updated.astype(jnp.bfloat16)
                term = weight[:, r : r + 1] * parts[r, ROWS : 2 * ROWS, :].astype(jnp.float32)
                shared = term if shared is None else shared + term
            at = lanes(group * OWN + SLOTS)
            shared = shared.astype(jnp.bfloat16).astype(jnp.float32)
            out[:, at] = (residual[:, at].astype(jnp.float32) + shared).astype(jnp.bfloat16)


def whole(count):
    return [pl.BlockSpec(memory_space=VMEM)] * count


def on_device(
    planes, queries, keys, values, residual, q_gain, k_gain, gate_table, levels, offsets, incoming
):
    smem = pl.BlockSpec(memory_space=pltpu.SMEM)
    dests = SLOTS * GROUPS
    exchange = lambda x: lax.all_to_all(x, ("slot", "group"), 0, 0, tiled=True)
    up = [(z, z + 1) for z in range(planes - 1)]
    down = [(z + 1, z) for z in range(planes - 1)]
    count = planes * SLOTS

    kv = pl.pallas_call(
        pack_kv_kernel,
        out_shape=jax.ShapeDtypeStruct((dests, KV_ROWS, HD), jnp.bfloat16),
        in_specs=[HBM, HBM] + whole(1),
        out_specs=HBM,
        scratch_shapes=[
            VMEM(keys.shape[1:], jnp.bfloat16),
            VMEM(keys.shape[1:], jnp.bfloat16),
            VMEM((dests, KV_ROWS, HD), jnp.bfloat16),
            pltpu.SemaphoreType.DMA((2 * ROWS // CHUNK,)),
            pltpu.SemaphoreType.DMA((SLOTS,)),
        ],
        compiler_params=params(62),
        cost_estimate=pl.CostEstimate(flops=1_000_000, bytes_accessed=40_000_000, transcendentals=0),
        name="pack_kv",
    )(keys[0], values[0], k_gain[None])
    kv = exchange(kv)
    climbed = lax.ppermute(
        residual[0],
        ("plane", "slot"),
        [(z * SLOTS + SLOTS - 1, (z + 1) * SLOTS + SLOTS - 1) for z in range(planes - 1)],
    )
    queries, climbed = lax.optimization_barrier((queries, climbed))
    packed = pl.pallas_call(
        pack_q_kernel,
        out_shape=jax.ShapeDtypeStruct((dests, Q_ROWS, HD), jnp.bfloat16),
        in_specs=[smem] + whole(2),
        out_specs=whole(1)[0],
        compiler_params=params(),
        name="pack_q",
    )(levels, queries[0], q_gain[None])
    query = exchange(packed)
    shifted = jnp.where(lax.axis_index("slot") == SLOTS - 1, climbed, residual[0])
    query, shifted = lax.optimization_barrier((query, shifted))
    moved = lax.ppermute(shifted, "slot", [(i, (i + 1) % SLOTS) for i in range(SLOTS)])
    edge = REACH * GROUPS
    right = lax.ppermute(kv[:edge], "plane", down)
    left = lax.ppermute(kv[dests - edge :], "plane", up)

    def attend(frames, first_out, slots_out, name):
        blocks = 2 * REACH + SLOTS
        units = len(frames)
        return pl.pallas_call(
            functools.partial(attend_kernel, frames, first_out, planes, 256),
            out_shape=jax.ShapeDtypeStruct((slots_out * GROUPS, O_ROWS, HD), jnp.bfloat16),
            in_specs=[smem] + whole(5),
            out_specs=HBM,
            scratch_shapes=[
                VMEM((blocks, ROWS * GROUPS, HD), jnp.bfloat16),
                VMEM((blocks, ROWS * GROUPS, 2 * HD), jnp.bfloat16),
                VMEM((blocks, PART * GROUPS, HD), jnp.bfloat16),
                VMEM((blocks, PART * GROUPS, 2 * HD), jnp.bfloat16),
                VMEM((units * GROUPS, O_ROWS, HD), jnp.bfloat16),
                pltpu.SemaphoreType.DMA((units,)),
            ],
            compiler_params=params(),
            cost_estimate=pl.CostEstimate(
                flops=units * 500_000_000, bytes_accessed=4_000_000, transcendentals=units * 1_000_000
            ),
            name=name,
        )(offsets, left, kv, right, query, gate_table)

    last = attend((SLOTS - 1,), 0, 1, "attend_last")
    last = lax.ppermute(last, "plane", up)
    others = attend(tuple(range(SLOTS - 1)), 1, SLOTS, "attend_others")
    others, moved = lax.optimization_barrier((others, moved))
    parts = exchange(lax.dynamic_update_slice(others, last, (0, 0, 0)))
    updated = pl.pallas_call(
        combine_kernel,
        out_shape=jax.ShapeDtypeStruct(incoming.shape, jnp.bfloat16),
        in_specs=whole(3),
        out_specs=whole(1)[0],
        compiler_params=params(),
        name="combine",
    )(parts, moved, incoming)
    return updated[None]


def solution(mesh):
    planes = mesh.shape["frame"] // SLOTS
    inner = Mesh(
        mesh.devices.reshape(planes, SLOTS, GROUPS), ("plane", "slot", "group")
    )
    frame = ("plane", "slot")
    tokens = P(frame, "group", None)
    placed = (
        tokens,
        tokens,
        tokens,
        tokens,
        P(),
        P(),
        P(None, "group"),
        P(frame),
        P(frame),
        P("group", None),
    )
    return jax.shard_map(
        functools.partial(on_device, planes), mesh=inner, in_specs=placed, out_specs=tokens, check_vma=False
    )
```

```python
import functools
import math
import jax
import jax.numpy as jnp
from jax import lax
from jax.experimental import pallas as pl
from jax.experimental.pallas import tpu as pltpu
from jax.sharding import Mesh, PartitionSpec as P

HD = 128
W = 3
REACH = W - 1
SLOTS = 4
GROUPS = 8
OWN = 5
ROWS = 64
PART = ROWS // SLOTS
KV_ROWS = 2 * (ROWS + PART)
Q_ROWS = 2 * ROWS + 16
O_ROWS = 2 * ROWS + 16
SCALE = math.log2(math.e) / math.sqrt(HD)
FAR = 1e30
VMEM = pltpu.VMEM
HBM = pl.BlockSpec(memory_space=pltpu.HBM)


def params(mib=48):
    return pltpu.CompilerParams(vmem_limit_bytes=mib * 1024 * 1024)


def lanes(head):
    return slice(head * HD, (head + 1) * HD)


def scale_of(wide):
    return lax.rsqrt(jnp.mean(wide * wide, axis=-1, keepdims=True) + 1e-06)


def pack_kv_kernel(keys_in, values_in, gain, out, keys, values, blocks, in_sems, out_sems):
    reads = [
        pltpu.make_async_copy(source, target, in_sems.at[n])
        for n, (source, target) in enumerate(((values_in, values), (keys_in, keys)))
    ]
    for read in reads:
        read.start()
    writes = []

    def spread(make, base):
        for group in range(GROUPS):
            block = make(lanes(group * OWN + SLOTS))
            for slot in range(SLOTS):
                part = slice(slot * PART, (slot + 1) * PART)
                blocks[slot * GROUPS + group, base + ROWS : base + ROWS + PART, :] = block[part]
        for slot in range(SLOTS):
            for group in range(GROUPS):
                blocks[slot * GROUPS + group, base : base + ROWS, :] = make(lanes(group * OWN + slot))
            at = pl.ds(slot * GROUPS, GROUPS), pl.ds(base, ROWS + PART)
            write = pltpu.make_async_copy(blocks.at[at], out.at[at], out_sems.at[len(writes)])
            write.start()
            writes.append(write)

    reads[0].wait()
    spread(lambda at: values[:, at], ROWS + PART)
    reads[1].wait()
    by = scale_of(keys[...].astype(jnp.float32))
    spread(lambda at: (keys[:, at].astype(jnp.float32) * by * gain[:, at]).astype(jnp.bfloat16), 0)
    for write in writes:
        write.wait()


def pack_q_kernel(levels, queries, gain, out):
    by = scale_of(queries[...].astype(jnp.float32))
    level = jnp.full((16, HD), levels[0], jnp.int32).astype(jnp.float32).astype(jnp.bfloat16)
    for group in range(GROUPS):
        for own in range(OWN):
            at = lanes(group * OWN + own)
            query = (queries[:, at].astype(jnp.float32) * by * gain[:, at]).astype(jnp.bfloat16)
            if own < SLOTS:
                out[own * GROUPS + group, 0:ROWS, :] = query
                out[own * GROUPS + group, 2 * ROWS : Q_ROWS, :] = level
            else:
                for slot in range(SLOTS):
                    out[slot * GROUPS + group, ROWS : 2 * ROWS, :] = query


def attend_kernel(
    frames, first_out, planes, tile, offsets, mine, right, queries, gates, left_in, out_ref, key_all, value_all, key_part, value_part, out, sems, left, left_sem
):
    plane = lax.axis_index("plane")
    slot = lax.axis_index("slot")
    count = planes * SLOTS
    phase = lax.rem(offsets[0] + W * count - (plane * SLOTS + slot), W)
    ones = jnp.ones((ROWS * GROUPS, HD), jnp.bfloat16)
    below = None
    if left_in is not None:
        below = pltpu.make_async_copy(left_in, left, left_sem.at[0])
        below.start()
    unpacked = set()

    def unpack(j):
        if j in unpacked:
            return
        unpacked.add(j)
        if j < REACH:
            if not waited:
                below.wait()
                waited.append(True)
            ref, base = left, j * GROUPS
        elif j < REACH + SLOTS:
            ref, base = mine, (j - REACH) * GROUPS
        else:
            ref, base = right, (j - REACH - SLOTS) * GROUPS
        from_all = slice(base, base + GROUPS)
        key_all[j] = ref[from_all, 0:ROWS, :].reshape(ROWS * GROUPS, HD)
        key_part[j] = ref[from_all, ROWS : ROWS + PART, :].reshape(PART * GROUPS, HD)
        value_all[j, :, 0:HD] = ref[from_all, ROWS + PART : 2 * ROWS + PART, :].reshape(ROWS * GROUPS, HD)
        value_all[j, :, HD:] = ones
        value_part[j, :, 0:HD] = ref[from_all, 2 * ROWS + PART : KV_ROWS, :].reshape(PART * GROUPS, HD)
        value_part[j, :, HD:] = ones[: PART * GROUPS]

    waited = []

    def softmaxed(query, key_ref, value_ref, start, allowed):
        scores = [
            lax.dot_general(
                query, key_ref[start + b], (((1,), (1,)), ((), ())), preferred_element_type=jnp.float32
            )
            for b in range(W)
        ]
        tops = [
            jnp.where(
                allowed[b],
                functools.reduce(
                    jnp.maximum, [scores[b][:, lanes(n)] for n in range(scores[b].shape[1] // HD)]
                ),
                -FAR,
            )
            for b in range(W)
        ]
        top = jnp.max(functools.reduce(jnp.maximum, tops), axis=-1, keepdims=True)
        total = None
        for b in range(W):
            weights = jnp.exp2((scores[b] - jnp.where(allowed[b], top, FAR)) * SCALE)
            term = jnp.dot(
                weights.astype(jnp.bfloat16), value_ref[start + b], preferred_element_type=jnp.float32
            )
            total = term if total is None else total + term
        return top, total[:, :HD], total[:, HD:]

    row = lax.broadcasted_iota(jnp.int32, (16, HD), 0)
    level_row = lax.broadcasted_iota(jnp.int32, (gates.shape[0], HD), 0).astype(jnp.float32)
    spot = lax.broadcasted_iota(jnp.int32, (ROWS * GROUPS, HD), 0) % ROWS == lax.broadcasted_iota(
        jnp.int32, (ROWS * GROUPS, HD), 1
    )
    blocks_of = tile // ROWS
    writes = []
    for i in reversed(frames):
        for j in range(i + 2 * REACH, i - 1, -1):
            unpack(j)
        frame = plane * SLOTS + i
        offset = lax.rem(frame + phase, W)
        start = i + REACH - offset
        allowed = [
            (frame - offset + b >= 0) & (frame - offset + b < count) for b in range(W)
        ]
        level = queries[i * GROUPS, 2 * ROWS : 2 * ROWS + 1, :].astype(jnp.float32)
        picked = level_row == level

        def gate_of(at):
            return jnp.sum(jnp.where(picked, gates[:, at], 0.0), axis=0, keepdims=True)

        gate = gate_of(pl.ds(pl.multiple_of(slot * HD, HD), HD))
        gate_shared = gate_of(pl.ds(SLOTS * HD, HD))
        to = (i - frames[0]) * GROUPS

        for n in range(ROWS * GROUPS // tile):
            first = i * GROUPS + n * blocks_of
            query = queries[first : first + blocks_of, 0:ROWS, :].reshape(tile, HD)
            _, numer, total = softmaxed(query, key_all, value_all, start, allowed)
            done = (numer / total * gate).astype(jnp.bfloat16).reshape(blocks_of, ROWS, HD)
            first = to + n * blocks_of
            out[first : first + blocks_of, 0:ROWS, :] = done

        query = queries[i * GROUPS : (i + 1) * GROUPS, ROWS : 2 * ROWS, :].reshape(ROWS * GROUPS, HD)
        top, numer, total = softmaxed(query, key_part, value_part, start, allowed)
        done = (numer / total * gate_shared).astype(jnp.bfloat16).reshape(GROUPS, ROWS, HD)
        out[to : to + GROUPS, ROWS : 2 * ROWS, :] = done
        weight = top * SCALE + jnp.log2(total)
        weight = jnp.where(spot, weight, 0.0).reshape(GROUPS, ROWS, HD).sum(axis=1)
        high = weight.astype(jnp.bfloat16).astype(jnp.float32)
        rest = weight - high
        middle = rest.astype(jnp.bfloat16).astype(jnp.float32)
        low = rest - middle
        for t in range(GROUPS):
            at = slice(t, t + 1)
            three = jnp.where(row == 0, high[at], jnp.where(row == 1, middle[at], low[at]))
            out[to + t, 2 * ROWS : O_ROWS, :] = three.astype(jnp.bfloat16)
        write = pltpu.make_async_copy(
            out.at[pl.ds(to, GROUPS)],
            out_ref.at[pl.ds(to + first_out * GROUPS, GROUPS)],
            sems.at[i - frames[0]],
        )
        write.start()
        writes.append(write)
    for write in writes:
        write.wait()


def combine_kernel(parts, residual, incoming, out_ref, out, sems):
    first = (lax.axis_index("plane") == 0) & (lax.axis_index("slot") == 0)

    @pl.when(first)
    def _():
        write = pltpu.make_async_copy(incoming, out_ref, sems.at[0])
        write.start()
        write.wait()

    @pl.when(jnp.logical_not(first))
    def _():
        sent = parts[:, 2 * ROWS : O_ROWS, :].astype(jnp.float32)
        row = lax.broadcasted_iota(jnp.int32, sent.shape, 1)
        weight = jnp.sum(jnp.where(row < 3, sent, 0.0), axis=1).reshape(SLOTS, GROUPS, HD)
        weight = jnp.exp2(weight - jnp.max(weight, axis=0, keepdims=True))
        weight = weight / jnp.sum(weight, axis=0, keepdims=True)
        weight = weight.reshape(SLOTS * GROUPS, HD)
        weight = jnp.concatenate([weight, jnp.zeros((HD - SLOTS * GROUPS, HD), jnp.float32)])
        weight = weight.T[:ROWS]
        writes = []
        for group in range(GROUPS):
            shared = None
            for slot in range(SLOTS):
                r = slot * GROUPS + group
                at = lanes(group * OWN + slot)
                updated = residual[:, at].astype(jnp.float32) + parts[r, 0:ROWS, :].astype(jnp.float32)
                out[:, at] = updated.astype(jnp.bfloat16)
                term = weight[:, r : r + 1] * parts[r, ROWS : 2 * ROWS, :].astype(jnp.float32)
                shared = term if shared is None else shared + term
            at = lanes(group * OWN + SLOTS)
            shared = shared.astype(jnp.bfloat16).astype(jnp.float32)
            out[:, at] = (residual[:, at].astype(jnp.float32) + shared).astype(jnp.bfloat16)
            if group % 2:
                at = pl.ds((group - 1) * OWN * HD, 2 * OWN * HD)
                write = pltpu.make_async_copy(out.at[:, at], out_ref.at[:, at], sems.at[group // 2])
                write.start()
                writes.append(write)
        for write in writes:
            write.wait()


def whole(count):
    return [pl.BlockSpec(memory_space=VMEM)] * count


def on_device(
    planes, queries, keys, values, residual, q_gain, k_gain, gate_table, levels, offsets, incoming
):
    smem = pl.BlockSpec(memory_space=pltpu.SMEM)
    dests = SLOTS * GROUPS
    exchange = lambda x: lax.all_to_all(x, ("slot", "group"), 0, 0, tiled=True)
    up = [(z, z + 1) for z in range(planes - 1)]
    down = [(z + 1, z) for z in range(planes - 1)]
    count = planes * SLOTS

    kv = pl.pallas_call(
        pack_kv_kernel,
        out_shape=jax.ShapeDtypeStruct((dests, KV_ROWS, HD), jnp.bfloat16),
        in_specs=[HBM, HBM] + whole(1),
        out_specs=HBM,
        scratch_shapes=[
            VMEM(keys.shape[1:], jnp.bfloat16),
            VMEM(keys.shape[1:], jnp.bfloat16),
            VMEM((dests, KV_ROWS, HD), jnp.bfloat16),
            pltpu.SemaphoreType.DMA((2,)),
            pltpu.SemaphoreType.DMA((2 * SLOTS,)),
        ],
        compiler_params=params(62),
        cost_estimate=pl.CostEstimate(flops=1_000_000, bytes_accessed=40_000_000, transcendentals=0),
        name="pack_kv",
    )(keys[0], values[0], k_gain[None])
    kv = exchange(kv)
    climbed = lax.ppermute(
        residual[0],
        ("plane", "slot"),
        [(z * SLOTS + SLOTS - 1, (z + 1) * SLOTS + SLOTS - 1) for z in range(planes - 1)],
    )
    queries, climbed = lax.optimization_barrier((queries, climbed))
    packed = pl.pallas_call(
        pack_q_kernel,
        out_shape=jax.ShapeDtypeStruct((dests, Q_ROWS, HD), jnp.bfloat16),
        in_specs=[smem] + whole(2),
        out_specs=whole(1)[0],
        compiler_params=params(),
        name="pack_q",
    )(levels, queries[0], q_gain[None])
    query = exchange(packed)
    shifted = jnp.where(lax.axis_index("slot") == SLOTS - 1, climbed, residual[0])
    query, shifted = lax.optimization_barrier((query, shifted))
    moved = lax.ppermute(shifted, "slot", [(i, (i + 1) % SLOTS) for i in range(SLOTS)])
    edge = REACH * GROUPS
    right = lax.ppermute(kv[:edge], "plane", down)
    left = lax.ppermute(kv[dests - edge :], "plane", up)
    def attend(frames, first_out, slots_out, name):
        blocks = 2 * REACH + SLOTS
        units = len(frames)
        below = [left] if min(frames) < REACH else []

        def kernel(*refs):
            fixed, rest = refs[:5], refs[5:]
            attend_kernel(frames, first_out, planes, 256, *fixed, *(rest if below else (None, *rest)))

        return pl.pallas_call(
            kernel,
            out_shape=jax.ShapeDtypeStruct((slots_out * GROUPS, O_ROWS, HD), jnp.bfloat16),
            in_specs=[smem] + whole(4) + [HBM] * len(below),
            out_specs=HBM,
            scratch_shapes=[
                VMEM((blocks, ROWS * GROUPS, HD), jnp.bfloat16),
                VMEM((blocks, ROWS * GROUPS, 2 * HD), jnp.bfloat16),
                VMEM((blocks, PART * GROUPS, HD), jnp.bfloat16),
                VMEM((blocks, PART * GROUPS, 2 * HD), jnp.bfloat16),
                VMEM((units * GROUPS, O_ROWS, HD), jnp.bfloat16),
                pltpu.SemaphoreType.DMA((units,)),
                VMEM((edge, KV_ROWS, HD), jnp.bfloat16),
                pltpu.SemaphoreType.DMA((1,)),
            ],
            compiler_params=params(32),
            cost_estimate=pl.CostEstimate(
                flops=units * 500_000_000, bytes_accessed=4_000_000, transcendentals=units * 1_000_000
            ),
            name=name,
        )(offsets, kv, right, query, gate_table, *below)

    last = attend((SLOTS - 1,), 0, 1, "attend_last")
    last = lax.ppermute(last, "plane", up)
    others = attend(tuple(range(SLOTS - 1)), 1, SLOTS, "attend_others")
    others, moved = lax.optimization_barrier((others, moved))
    parts = exchange(lax.dynamic_update_slice(others, last, (0, 0, 0)))
    updated = pl.pallas_call(
        combine_kernel,
        out_shape=jax.ShapeDtypeStruct(incoming.shape, jnp.bfloat16),
        in_specs=whole(3),
        out_specs=HBM,
        scratch_shapes=[VMEM(incoming.shape, jnp.bfloat16), pltpu.SemaphoreType.DMA((GROUPS // 2,))],
        compiler_params=params(),
        name="combine",
    )(parts, moved, incoming)
    return updated[None]


def solution(mesh):
    planes = mesh.shape["frame"] // SLOTS
    inner = Mesh(
        mesh.devices.reshape(planes, SLOTS, GROUPS), ("plane", "slot", "group")
    )
    frame = ("plane", "slot")
    tokens = P(frame, "group", None)
    placed = (
        tokens,
        tokens,
        tokens,
        tokens,
        P(),
        P(),
        P(None, "group"),
        P(frame),
        P(frame),
        P("group", None),
    )
    return jax.shard_map(
        functools.partial(on_device, planes), mesh=inner, in_specs=placed, out_specs=tokens, check_vma=False
    )
```

```python
import functools
import math
import jax
import jax.numpy as jnp
from jax import lax
from jax.experimental import pallas as pl
from jax.experimental.pallas import tpu as pltpu
from jax.sharding import Mesh, PartitionSpec as P

HD = 128
W = 3
SLOTS = 4
BELOW = 3
ABOVE = 1
GROUPS = 8
OWN = 5
ROWS = 64
PART = ROWS // SLOTS
KV_ROWS = 2 * (ROWS + PART)
Q_ROWS = 2 * ROWS + 16
O_ROWS = 2 * ROWS + 16
SCALE = math.log2(math.e) / math.sqrt(HD)
FAR = 1e30
VMEM = pltpu.VMEM
HBM = pl.BlockSpec(memory_space=pltpu.HBM)


def params(mib=48):
    return pltpu.CompilerParams(vmem_limit_bytes=mib * 1024 * 1024)


def lanes(head):
    return slice(head * HD, (head + 1) * HD)


def scale_of(wide):
    return lax.rsqrt(jnp.mean(wide * wide, axis=-1, keepdims=True) + 1e-06)


def pack_kv_kernel(keys_in, values_in, gain, out, keys, values, blocks, in_sems, out_sems):
    reads = [
        pltpu.make_async_copy(source, target, in_sems.at[n])
        for n, (source, target) in enumerate(((values_in, values), (keys_in, keys)))
    ]
    for read in reads:
        read.start()
    writes = []

    def spread(make, base):
        for group in range(GROUPS):
            block = make(lanes(group * OWN + SLOTS))
            for slot in range(SLOTS):
                part = slice(slot * PART, (slot + 1) * PART)
                blocks[slot * GROUPS + group, base + ROWS : base + ROWS + PART, :] = block[part]
        for slot in range(SLOTS):
            for group in range(GROUPS):
                blocks[slot * GROUPS + group, base : base + ROWS, :] = make(lanes(group * OWN + slot))
            at = pl.ds(slot * GROUPS, GROUPS), pl.ds(base, ROWS + PART)
            write = pltpu.make_async_copy(blocks.at[at], out.at[at], out_sems.at[len(writes)])
            write.start()
            writes.append(write)

    reads[0].wait()
    spread(lambda at: values[:, at], ROWS + PART)
    reads[1].wait()
    by = scale_of(keys[...].astype(jnp.float32))
    spread(lambda at: (keys[:, at].astype(jnp.float32) * by * gain[:, at]).astype(jnp.bfloat16), 0)
    for write in writes:
        write.wait()


def pack_q_kernel(levels, own, climbed, gain, out):
    last = lax.axis_index("slot") == SLOTS - 1
    width = own.shape[1]

    def spread(queries, info):
        by = scale_of(queries[:, :width].astype(jnp.float32))
        for group in range(GROUPS):
            for part in range(OWN):
                at = lanes(group * OWN + part)
                query = (queries[:, at].astype(jnp.float32) * by * gain[:, at]).astype(jnp.bfloat16)
                if part < SLOTS:
                    out[part * GROUPS + group, 0:ROWS, :] = query
                    out[part * GROUPS + group, 2 * ROWS : Q_ROWS, :] = info
                else:
                    for slot in range(SLOTS):
                        out[slot * GROUPS + group, ROWS : 2 * ROWS, :] = query

    @pl.when(last)
    def _():
        spread(climbed, climbed[0:16, width:])

    @pl.when(jnp.logical_not(last))
    def _():
        spread(own, jnp.full((16, HD), levels[0], jnp.int32).astype(jnp.float32).astype(jnp.bfloat16))


def attend_kernel(
    frames, spans, places, copied, planes, tile, offsets, mine, queries, gates, *refs
):
    edges, refs = refs[: len(spans)], refs[len(spans) :]
    earlier, refs = refs[: len(places) - 1], refs[len(places) - 1 :]
    out_ref, key_all, value_all, key_part, value_part, out, sems, done_sems, edge_sem, *room = refs
    reads = []
    if copied:
        reads.append(pltpu.make_async_copy(edges[0], room[0], edge_sem.at[0]))
        reads[0].start()
        edges = (room[0], *edges[1:])
    plane = lax.axis_index("plane")
    slot = lax.axis_index("slot")
    count = planes * SLOTS
    phase = lax.rem(offsets[0] + W * count - (plane * SLOTS + slot), W)
    ones = jnp.ones((ROWS * GROUPS, HD), jnp.bfloat16)
    writes = []
    for n, (done, place) in enumerate(zip(earlier, places[1:])):
        write = pltpu.make_async_copy(
            done, out_ref.at[pl.ds(place * GROUPS, done.shape[0])], done_sems.at[n]
        )
        write.start()
        writes.append(write)
    unpacked = set()

    def unpack(j):
        if j in unpacked:
            return
        unpacked.add(j)
        if BELOW <= j < BELOW + SLOTS:
            ref, base = mine, (j - BELOW) * GROUPS
        else:
            n = next(
                n for n, span in enumerate(spans) if span <= j < span + edges[n].shape[0] // GROUPS
            )
            ref, base = edges[n], (j - spans[n]) * GROUPS
            if n == 0 and reads:
                reads.pop().wait()
        from_all = slice(base, base + GROUPS)
        key_all[j] = ref[from_all, 0:ROWS, :].reshape(ROWS * GROUPS, HD)
        key_part[j] = ref[from_all, ROWS : ROWS + PART, :].reshape(PART * GROUPS, HD)
        value_all[j, :, 0:HD] = ref[from_all, ROWS + PART : 2 * ROWS + PART, :].reshape(ROWS * GROUPS, HD)
        value_all[j, :, HD:] = ones
        value_part[j, :, 0:HD] = ref[from_all, 2 * ROWS + PART : KV_ROWS, :].reshape(PART * GROUPS, HD)
        value_part[j, :, HD:] = ones[: PART * GROUPS]

    def softmaxed(query, key_ref, value_ref, start, allowed):
        scores = [
            lax.dot_general(
                query, key_ref[start + b], (((1,), (1,)), ((), ())), preferred_element_type=jnp.float32
            )
            for b in range(W)
        ]
        tops = [
            jnp.where(
                allowed[b],
                functools.reduce(
                    jnp.maximum, [scores[b][:, lanes(n)] for n in range(scores[b].shape[1] // HD)]
                ),
                -FAR,
            )
            for b in range(W)
        ]
        top = jnp.max(functools.reduce(jnp.maximum, tops), axis=-1, keepdims=True)
        total = None
        for b in range(W):
            weights = jnp.exp2((scores[b] - jnp.where(allowed[b], top, FAR)) * SCALE)
            term = jnp.dot(
                weights.astype(jnp.bfloat16), value_ref[start + b], preferred_element_type=jnp.float32
            )
            total = term if total is None else total + term
        return top, total[:, :HD], total[:, HD:]

    row = lax.broadcasted_iota(jnp.int32, (16, HD), 0)
    level_row = lax.broadcasted_iota(jnp.int32, (gates.shape[0], HD), 0).astype(jnp.float32)
    spot = lax.broadcasted_iota(jnp.int32, (ROWS * GROUPS, HD), 0) % ROWS == lax.broadcasted_iota(
        jnp.int32, (ROWS * GROUPS, HD), 1
    )
    blocks_of = tile // ROWS
    for i in reversed(frames):
        for j in sorted(
            range(i + BELOW - W + 1, i + BELOW + W),
            key=lambda j: (copied and spans[0] <= j < spans[0] + edges[0].shape[0] // GROUPS, -j),
        ):
            unpack(j)
        frame = plane * SLOTS + i
        offset = lax.rem(frame + W + phase, W)
        start = i + BELOW - offset
        allowed = [
            (frame < 0) | (frame - offset + b >= 0) & (frame - offset + b < count) for b in range(W)
        ]
        at_slot = i % SLOTS
        level = queries[at_slot * GROUPS, 2 * ROWS : 2 * ROWS + 1, :].astype(jnp.float32)
        picked = level_row == level

        def gate_of(at):
            return jnp.sum(jnp.where(picked, gates[:, at], 0.0), axis=0, keepdims=True)

        gate = gate_of(pl.ds(pl.multiple_of(slot * HD, HD), HD))
        gate_shared = gate_of(pl.ds(SLOTS * HD, HD))
        to = (i - frames[0]) * GROUPS

        for n in range(ROWS * GROUPS // tile):
            first = at_slot * GROUPS + n * blocks_of
            query = queries[first : first + blocks_of, 0:ROWS, :].reshape(tile, HD)
            _, numer, total = softmaxed(query, key_all, value_all, start, allowed)
            done = (numer / total * gate).astype(jnp.bfloat16).reshape(blocks_of, ROWS, HD)
            first = to + n * blocks_of
            out[first : first + blocks_of, 0:ROWS, :] = done

        query = queries[at_slot * GROUPS : (at_slot + 1) * GROUPS, ROWS : 2 * ROWS, :].reshape(ROWS * GROUPS, HD)
        top, numer, total = softmaxed(query, key_part, value_part, start, allowed)
        done = (numer / total * gate_shared).astype(jnp.bfloat16).reshape(GROUPS, ROWS, HD)
        out[to : to + GROUPS, ROWS : 2 * ROWS, :] = done
        weight = top * SCALE + jnp.log2(total)
        weight = jnp.where(spot, weight, 0.0).reshape(GROUPS, ROWS, HD).sum(axis=1)
        high = weight.astype(jnp.bfloat16).astype(jnp.float32)
        rest = weight - high
        middle = rest.astype(jnp.bfloat16).astype(jnp.float32)
        low = rest - middle
        for t in range(GROUPS):
            at = slice(t, t + 1)
            three = jnp.where(row == 0, high[at], jnp.where(row == 1, middle[at], low[at]))
            out[to + t, 2 * ROWS : O_ROWS, :] = three.astype(jnp.bfloat16)
        write = pltpu.make_async_copy(
            out.at[pl.ds(to, GROUPS)],
            out_ref.at[pl.ds(places[0] * GROUPS + to, GROUPS)],
            sems.at[i - frames[0]],
        )
        write.start()
        writes.append(write)
    for write in writes:
        write.wait()


def combine_kernel(parts, residual_in, incoming, out_ref, residual, out, sems, in_sems):
    first = (lax.axis_index("plane") == 0) & (lax.axis_index("slot") == 0)

    @pl.when(first)
    def _():
        write = pltpu.make_async_copy(incoming, out_ref, sems.at[0])
        write.start()
        write.wait()

    @pl.when(jnp.logical_not(first))
    def _():
        reads = []
        for n in range(GROUPS // 2):
            at = pl.ds(n * 2 * OWN * HD, 2 * OWN * HD)
            reads.append(pltpu.make_async_copy(residual_in.at[:, at], residual.at[:, at], in_sems.at[n]))
            reads[n].start()
        sent = parts[:, 2 * ROWS : O_ROWS, :].astype(jnp.float32)
        row = lax.broadcasted_iota(jnp.int32, sent.shape, 1)
        weight = jnp.sum(jnp.where(row < 3, sent, 0.0), axis=1).reshape(SLOTS, GROUPS, HD)
        weight = jnp.exp2(weight - jnp.max(weight, axis=0, keepdims=True))
        weight = weight / jnp.sum(weight, axis=0, keepdims=True)
        weight = weight.reshape(SLOTS * GROUPS, HD)
        weight = jnp.concatenate([weight, jnp.zeros((HD - SLOTS * GROUPS, HD), jnp.float32)])
        weight = weight.T[:ROWS]
        writes = []
        for group in range(GROUPS):
            if group % 2 == 0:
                reads[group // 2].wait()
            shared = None
            for slot in range(SLOTS):
                r = slot * GROUPS + group
                at = lanes(group * OWN + slot)
                updated = residual[:, at].astype(jnp.float32) + parts[r, 0:ROWS, :].astype(jnp.float32)
                out[:, at] = updated.astype(jnp.bfloat16)
                term = weight[:, r : r + 1] * parts[r, ROWS : 2 * ROWS, :].astype(jnp.float32)
                shared = term if shared is None else shared + term
            at = lanes(group * OWN + SLOTS)
            shared = shared.astype(jnp.bfloat16).astype(jnp.float32)
            out[:, at] = (residual[:, at].astype(jnp.float32) + shared).astype(jnp.bfloat16)
            if group % 2:
                at = pl.ds((group - 1) * OWN * HD, 2 * OWN * HD)
                write = pltpu.make_async_copy(out.at[:, at], out_ref.at[:, at], sems.at[group // 2])
                write.start()
                writes.append(write)
        for write in writes:
            write.wait()


def whole(count):
    return [pl.BlockSpec(memory_space=VMEM)] * count


def on_device(
    planes, queries, keys, values, residual, q_gain, k_gain, gate_table, levels, offsets, incoming
):
    smem = pl.BlockSpec(memory_space=pltpu.SMEM)
    dests = SLOTS * GROUPS
    exchange = lambda x: lax.all_to_all(x, ("slot", "group"), 0, 0, tiled=True)
    up = [(z, z + 1) for z in range(planes - 1)]
    down = [(z + 1, z) for z in range(planes - 1)]

    kv = pl.pallas_call(
        pack_kv_kernel,
        out_shape=jax.ShapeDtypeStruct((dests, KV_ROWS, HD), jnp.bfloat16),
        in_specs=[HBM, HBM] + whole(1),
        out_specs=HBM,
        scratch_shapes=[
            VMEM(keys.shape[1:], jnp.bfloat16),
            VMEM(keys.shape[1:], jnp.bfloat16),
            VMEM((dests, KV_ROWS, HD), jnp.bfloat16),
            pltpu.SemaphoreType.DMA((2,)),
            pltpu.SemaphoreType.DMA((2 * SLOTS,)),
        ],
        compiler_params=params(62),
        cost_estimate=pl.CostEstimate(flops=1_000_000, bytes_accessed=40_000_000, transcendentals=0),
        name="pack_kv",
    )(keys[0], values[0], k_gain[None])
    kv = exchange(kv)
    last = SLOTS - 1
    climb = [(z * SLOTS + last, (z + 1) * SLOTS + last) for z in range(planes - 1)]
    level = jnp.broadcast_to(levels.astype(jnp.bfloat16), (ROWS, HD))
    climbed_queries, climbed = (
        lax.ppermute(x, ("plane", "slot"), climb)
        for x in (jnp.concatenate([queries[0], level], axis=1), residual[0])
    )
    packed = pl.pallas_call(
        pack_q_kernel,
        out_shape=jax.ShapeDtypeStruct((dests, Q_ROWS, HD), jnp.bfloat16),
        in_specs=[smem] + whole(3),
        out_specs=whole(1)[0],
        compiler_params=params(),
        name="pack_q",
    )(levels, queries[0], climbed_queries, q_gain[None])
    kv, climbed = lax.optimization_barrier((kv, climbed))
    query = exchange(packed)
    near = lax.ppermute(kv[2 * GROUPS :], "plane", up)
    right = lax.ppermute(kv[:GROUPS], "plane", down)
    far = lax.ppermute(kv[GROUPS : 2 * GROUPS], "plane", up)

    def attend(frames, edges, place, earlier, slots_out, name, copied=True):
        blocks = BELOW + SLOTS + ABOVE
        units = len(frames)
        return pl.pallas_call(
            functools.partial(
                attend_kernel,
                frames,
                [span for span, _ in edges],
                [place] + [at for at, _ in earlier],
                copied,
                planes,
                256,
            ),
            out_shape=jax.ShapeDtypeStruct((slots_out * GROUPS, O_ROWS, HD), jnp.bfloat16),
            in_specs=[smem] + whole(3) + [HBM] * copied + whole(len(edges) - copied + len(earlier)),
            out_specs=HBM,
            scratch_shapes=[
                VMEM((blocks, ROWS * GROUPS, HD), jnp.bfloat16),
                VMEM((blocks, ROWS * GROUPS, 2 * HD), jnp.bfloat16),
                VMEM((blocks, PART * GROUPS, HD), jnp.bfloat16),
                VMEM((blocks, PART * GROUPS, 2 * HD), jnp.bfloat16),
                VMEM((units * GROUPS, O_ROWS, HD), jnp.bfloat16),
                pltpu.SemaphoreType.DMA((units,)),
                pltpu.SemaphoreType.DMA((2,)),
                pltpu.SemaphoreType.DMA((1,)),
            ]
            + [VMEM(edges[0][1].shape, jnp.bfloat16)] * copied,
            compiler_params=params(32),
            cost_estimate=pl.CostEstimate(
                flops=units * 500_000_000, bytes_accessed=4_000_000, transcendentals=units * 1_000_000
            ),
            name=name,
        )(offsets, kv, query, gate_table, *(x for _, x in edges), *(x for _, x in earlier))

    shifted = jnp.where(lax.axis_index("slot") == last, climbed, residual[0])
    moved = lax.ppermute(shifted, "slot", [(i, (i + 1) % SLOTS) for i in range(SLOTS)])
    inner = attend((0, 1), [(1, near)], 0, [], 2, "attend_inner", False)
    inner, query = lax.optimization_barrier((inner, query))
    upper = attend((2,), [(BELOW + SLOTS, right)], 0, [], 1, "attend_upper")
    upper, query = lax.optimization_barrier((upper, query))
    attended = attend((-1,), [(0, far), (1, near)], 0, [(1, inner), (3, upper)], SLOTS, "attend_lower")
    attended, moved = lax.optimization_barrier((attended, moved))
    parts = exchange(attended)
    updated = pl.pallas_call(
        combine_kernel,
        out_shape=jax.ShapeDtypeStruct(incoming.shape, jnp.bfloat16),
        in_specs=[pl.BlockSpec(memory_space=VMEM), HBM, pl.BlockSpec(memory_space=VMEM)],
        out_specs=HBM,
        scratch_shapes=[
            VMEM(incoming.shape, jnp.bfloat16),
            VMEM(incoming.shape, jnp.bfloat16),
            pltpu.SemaphoreType.DMA((GROUPS // 2,)),
            pltpu.SemaphoreType.DMA((GROUPS // 2,)),
        ],
        compiler_params=params(20),
        cost_estimate=pl.CostEstimate(flops=1_000, bytes_accessed=4_000_000, transcendentals=0),
        name="combine",
    )(parts, moved, incoming)
    return updated[None]


def solution(mesh):
    planes = mesh.shape["frame"] // SLOTS
    inner = Mesh(
        mesh.devices.reshape(planes, SLOTS, GROUPS), ("plane", "slot", "group")
    )
    frame = ("plane", "slot")
    tokens = P(frame, "group", None)
    placed = (
        tokens,
        tokens,
        tokens,
        tokens,
        P(),
        P(),
        P(None, "group"),
        P(frame),
        P(frame),
        P("group", None),
    )
    return jax.shard_map(
        functools.partial(on_device, planes), mesh=inner, in_specs=placed, out_specs=tokens, check_vma=False
    )
```

```python
import functools
import math
import jax
import jax.numpy as jnp
from jax import lax
from jax.experimental import pallas as pl
from jax.experimental.pallas import tpu as pltpu
from jax.sharding import Mesh, PartitionSpec as P

HD = 128
W = 3
SLOTS = 4
BELOW = 3
ABOVE = 1
GROUPS = 8
OWN = 5
ROWS = 64
PART = ROWS // SLOTS
KV_ROWS = 2 * (ROWS + PART)
Q_ROWS = 2 * ROWS + 16
O_ROWS = 2 * ROWS + 16
SCALE = math.log2(math.e) / math.sqrt(HD)
FAR = 1e30
VMEM = pltpu.VMEM
HBM = pl.BlockSpec(memory_space=pltpu.HBM)


def params(mib=48):
    return pltpu.CompilerParams(vmem_limit_bytes=mib * 1024 * 1024)


def lanes(head):
    return slice(head * HD, (head + 1) * HD)


def scale_of(wide):
    return lax.rsqrt(jnp.mean(wide * wide, axis=-1, keepdims=True) + 1e-06)


def pack_kv_kernel(keys_in, values_in, gain, out, keys, values, blocks, in_sems, out_sems):
    reads = [
        pltpu.make_async_copy(source, target, in_sems.at[n])
        for n, (source, target) in enumerate(((values_in, values), (keys_in, keys)))
    ]
    for read in reads:
        read.start()
    writes = []

    def spread(make, base):
        for group in range(GROUPS):
            block = make(lanes(group * OWN + SLOTS))
            for slot in range(SLOTS):
                part = slice(slot * PART, (slot + 1) * PART)
                blocks[slot * GROUPS + group, base + ROWS : base + ROWS + PART, :] = block[part]
        for slot in range(SLOTS):
            for group in range(GROUPS):
                blocks[slot * GROUPS + group, base : base + ROWS, :] = make(lanes(group * OWN + slot))
            at = pl.ds(slot * GROUPS, GROUPS), pl.ds(base, ROWS + PART)
            write = pltpu.make_async_copy(blocks.at[at], out.at[at], out_sems.at[len(writes)])
            write.start()
            writes.append(write)

    reads[0].wait()
    spread(lambda at: values[:, at], ROWS + PART)
    reads[1].wait()
    by = scale_of(keys[...].astype(jnp.float32))
    spread(lambda at: (keys[:, at].astype(jnp.float32) * by * gain[:, at]).astype(jnp.bfloat16), 0)
    for write in writes:
        write.wait()


def pack_q_kernel(levels, own, climbed, gain, out):
    last = lax.axis_index("slot") == SLOTS - 1
    width = own.shape[1]

    def spread(queries, info):
        by = scale_of(queries[:, :width].astype(jnp.float32))
        for group in range(GROUPS):
            for part in range(OWN):
                at = lanes(group * OWN + part)
                query = (queries[:, at].astype(jnp.float32) * by * gain[:, at]).astype(jnp.bfloat16)
                if part < SLOTS:
                    out[part * GROUPS + group, 0:ROWS, :] = query
                    out[part * GROUPS + group, 2 * ROWS : Q_ROWS, :] = info
                else:
                    for slot in range(SLOTS):
                        out[slot * GROUPS + group, ROWS : 2 * ROWS, :] = query

    @pl.when(last)
    def _():
        spread(climbed, climbed[0:16, width:])

    @pl.when(jnp.logical_not(last))
    def _():
        spread(own, jnp.full((16, HD), levels[0], jnp.int32).astype(jnp.float32).astype(jnp.bfloat16))


def attend_kernel(
    frames, spans, places, copied, planes, tile, offsets, mine, queries, gates, *refs
):
    edges, refs = refs[: len(spans)], refs[len(spans) :]
    earlier, refs = refs[: len(places) - 1], refs[len(places) - 1 :]
    out_ref, key_all, value_all, key_part, value_part, out, sems, done_sems, edge_sem, *room = refs
    reads = []
    if copied:
        reads.append(pltpu.make_async_copy(edges[0], room[0], edge_sem.at[0]))
        reads[0].start()
        edges = (room[0], *edges[1:])
    plane = lax.axis_index("plane")
    slot = lax.axis_index("slot")
    count = planes * SLOTS
    phase = lax.rem(offsets[0] + W * count - (plane * SLOTS + slot), W)
    ones = jnp.ones((ROWS * GROUPS, HD), jnp.bfloat16)
    writes = []
    for n, (done, place) in enumerate(zip(earlier, places[1:])):
        write = pltpu.make_async_copy(
            done, out_ref.at[pl.ds(place * GROUPS, done.shape[0])], done_sems.at[n]
        )
        write.start()
        writes.append(write)
    unpacked = set()

    def unpack(j):
        if j in unpacked:
            return
        unpacked.add(j)
        if BELOW <= j < BELOW + SLOTS:
            ref, base = mine, (j - BELOW) * GROUPS
        else:
            n = next(
                n for n, span in enumerate(spans) if span <= j < span + edges[n].shape[0] // GROUPS
            )
            ref, base = edges[n], (j - spans[n]) * GROUPS
            if n == 0 and reads:
                reads.pop().wait()
        from_all = slice(base, base + GROUPS)
        key_all[j] = ref[from_all, 0:ROWS, :].reshape(ROWS * GROUPS, HD)
        key_part[j] = ref[from_all, ROWS : ROWS + PART, :].reshape(PART * GROUPS, HD)
        value_all[j, :, 0:HD] = ref[from_all, ROWS + PART : 2 * ROWS + PART, :].reshape(ROWS * GROUPS, HD)
        value_all[j, :, HD:] = ones
        value_part[j, :, 0:HD] = ref[from_all, 2 * ROWS + PART : KV_ROWS, :].reshape(PART * GROUPS, HD)
        value_part[j, :, HD:] = ones[: PART * GROUPS]

    def softmaxed(query, key_ref, value_ref, start, allowed):
        scores = [
            lax.dot_general(
                query, key_ref[start + b], (((1,), (1,)), ((), ())), preferred_element_type=jnp.float32
            )
            for b in range(W)
        ]
        tops = [
            jnp.where(
                allowed[b],
                functools.reduce(
                    jnp.maximum, [scores[b][:, lanes(n)] for n in range(scores[b].shape[1] // HD)]
                ),
                -FAR,
            )
            for b in range(W)
        ]
        top = jnp.max(functools.reduce(jnp.maximum, tops), axis=-1, keepdims=True)
        total = None
        for b in range(W):
            weights = jnp.exp2((scores[b] - jnp.where(allowed[b], top, FAR)) * SCALE)
            term = jnp.dot(
                weights.astype(jnp.bfloat16), value_ref[start + b], preferred_element_type=jnp.float32
            )
            total = term if total is None else total + term
        return top, total[:, :HD], total[:, HD:]

    row = lax.broadcasted_iota(jnp.int32, (16, HD), 0)
    level_row = lax.broadcasted_iota(jnp.int32, (gates.shape[0], HD), 0).astype(jnp.float32)
    spot = lax.broadcasted_iota(jnp.int32, (ROWS * GROUPS, HD), 0) % ROWS == lax.broadcasted_iota(
        jnp.int32, (ROWS * GROUPS, HD), 1
    )
    blocks_of = tile // ROWS
    for i in sorted(frames, key=lambda i: (i == SLOTS - 2, -i)):
        for j in sorted(
            range(i + BELOW - W + 1, i + BELOW + W),
            key=lambda j: (copied and spans[0] <= j < spans[0] + edges[0].shape[0] // GROUPS, -j),
        ):
            unpack(j)
        frame = plane * SLOTS + i
        offset = lax.rem(frame + W + phase, W)
        start = i + BELOW - offset
        allowed = [
            (frame < 0) | (frame - offset + b >= 0) & (frame - offset + b < count) for b in range(W)
        ]
        at_slot = i % SLOTS
        level = queries[at_slot * GROUPS, 2 * ROWS : 2 * ROWS + 1, :].astype(jnp.float32)
        picked = level_row == level

        def gate_of(at):
            return jnp.sum(jnp.where(picked, gates[:, at], 0.0), axis=0, keepdims=True)

        gate = gate_of(pl.ds(pl.multiple_of(slot * HD, HD), HD))
        gate_shared = gate_of(pl.ds(SLOTS * HD, HD))
        to = (i - frames[0]) * GROUPS

        for n in range(ROWS * GROUPS // tile):
            first = at_slot * GROUPS + n * blocks_of
            query = queries[first : first + blocks_of, 0:ROWS, :].reshape(tile, HD)
            _, numer, total = softmaxed(query, key_all, value_all, start, allowed)
            done = (numer / total * gate).astype(jnp.bfloat16).reshape(blocks_of, ROWS, HD)
            first = to + n * blocks_of
            out[first : first + blocks_of, 0:ROWS, :] = done

        query = queries[at_slot * GROUPS : (at_slot + 1) * GROUPS, ROWS : 2 * ROWS, :].reshape(ROWS * GROUPS, HD)
        top, numer, total = softmaxed(query, key_part, value_part, start, allowed)
        done = (numer / total * gate_shared).astype(jnp.bfloat16).reshape(GROUPS, ROWS, HD)
        out[to : to + GROUPS, ROWS : 2 * ROWS, :] = done
        weight = top * SCALE + jnp.log2(total)
        weight = jnp.where(spot, weight, 0.0).reshape(GROUPS, ROWS, HD).sum(axis=1)
        high = weight.astype(jnp.bfloat16).astype(jnp.float32)
        rest = weight - high
        middle = rest.astype(jnp.bfloat16).astype(jnp.float32)
        low = rest - middle
        for t in range(GROUPS):
            at = slice(t, t + 1)
            three = jnp.where(row == 0, high[at], jnp.where(row == 1, middle[at], low[at]))
            out[to + t, 2 * ROWS : O_ROWS, :] = three.astype(jnp.bfloat16)
        write = pltpu.make_async_copy(
            out.at[pl.ds(to, GROUPS)],
            out_ref.at[pl.ds(places[0] * GROUPS + to, GROUPS)],
            sems.at[i - frames[0]],
        )
        write.start()
        writes.append(write)
    for write in writes:
        write.wait()


def combine_kernel(parts, residual_in, incoming, out_ref, residual, out, sems, in_sems):
    first = (lax.axis_index("plane") == 0) & (lax.axis_index("slot") == 0)

    @pl.when(first)
    def _():
        write = pltpu.make_async_copy(incoming, out_ref, sems.at[0])
        write.start()
        write.wait()

    @pl.when(jnp.logical_not(first))
    def _():
        reads = []
        for n in range(GROUPS // 2):
            at = pl.ds(n * 2 * OWN * HD, 2 * OWN * HD)
            reads.append(pltpu.make_async_copy(residual_in.at[:, at], residual.at[:, at], in_sems.at[n]))
            reads[n].start()
        sent = parts[:, 2 * ROWS : O_ROWS, :].astype(jnp.float32)
        row = lax.broadcasted_iota(jnp.int32, sent.shape, 1)
        weight = jnp.sum(jnp.where(row < 3, sent, 0.0), axis=1).reshape(SLOTS, GROUPS, HD)
        weight = jnp.exp2(weight - jnp.max(weight, axis=0, keepdims=True))
        weight = weight / jnp.sum(weight, axis=0, keepdims=True)
        weight = weight.reshape(SLOTS * GROUPS, HD)
        weight = jnp.concatenate([weight, jnp.zeros((HD - SLOTS * GROUPS, HD), jnp.float32)])
        weight = weight.T[:ROWS]
        writes = []
        for group in range(GROUPS):
            if group % 2 == 0:
                reads[group // 2].wait()
            shared = None
            for slot in range(SLOTS):
                r = slot * GROUPS + group
                at = lanes(group * OWN + slot)
                updated = residual[:, at].astype(jnp.float32) + parts[r, 0:ROWS, :].astype(jnp.float32)
                out[:, at] = updated.astype(jnp.bfloat16)
                term = weight[:, r : r + 1] * parts[r, ROWS : 2 * ROWS, :].astype(jnp.float32)
                shared = term if shared is None else shared + term
            at = lanes(group * OWN + SLOTS)
            shared = shared.astype(jnp.bfloat16).astype(jnp.float32)
            out[:, at] = (residual[:, at].astype(jnp.float32) + shared).astype(jnp.bfloat16)
            if group % 2:
                at = pl.ds((group - 1) * OWN * HD, 2 * OWN * HD)
                write = pltpu.make_async_copy(out.at[:, at], out_ref.at[:, at], sems.at[group // 2])
                write.start()
                writes.append(write)
        for write in writes:
            write.wait()


def whole(count):
    return [pl.BlockSpec(memory_space=VMEM)] * count


def on_device(
    planes, queries, keys, values, residual, q_gain, k_gain, gate_table, levels, offsets, incoming
):
    smem = pl.BlockSpec(memory_space=pltpu.SMEM)
    dests = SLOTS * GROUPS
    exchange = lambda x: lax.all_to_all(x, ("slot", "group"), 0, 0, tiled=True)
    up = [(z, z + 1) for z in range(planes - 1)]
    down = [(z + 1, z) for z in range(planes - 1)]

    kv = pl.pallas_call(
        pack_kv_kernel,
        out_shape=jax.ShapeDtypeStruct((dests, KV_ROWS, HD), jnp.bfloat16),
        in_specs=[HBM, HBM] + whole(1),
        out_specs=HBM,
        scratch_shapes=[
            VMEM(keys.shape[1:], jnp.bfloat16),
            VMEM(keys.shape[1:], jnp.bfloat16),
            VMEM((dests, KV_ROWS, HD), jnp.bfloat16),
            pltpu.SemaphoreType.DMA((2,)),
            pltpu.SemaphoreType.DMA((2 * SLOTS,)),
        ],
        compiler_params=params(62),
        cost_estimate=pl.CostEstimate(flops=1_000_000, bytes_accessed=40_000_000, transcendentals=0),
        name="pack_kv",
    )(keys[0], values[0], k_gain[None])
    kv = exchange(kv)
    last = SLOTS - 1
    climb = [(z * SLOTS + last, (z + 1) * SLOTS + last) for z in range(planes - 1)]
    level = jnp.broadcast_to(levels.astype(jnp.bfloat16), (ROWS, HD))
    climbed_queries, climbed = (
        lax.ppermute(x, ("plane", "slot"), climb)
        for x in (jnp.concatenate([queries[0], level], axis=1), residual[0])
    )
    packed = pl.pallas_call(
        pack_q_kernel,
        out_shape=jax.ShapeDtypeStruct((dests, Q_ROWS, HD), jnp.bfloat16),
        in_specs=[smem] + whole(3),
        out_specs=whole(1)[0],
        compiler_params=params(),
        name="pack_q",
    )(levels, queries[0], climbed_queries, q_gain[None])
    kv, climbed = lax.optimization_barrier((kv, climbed))
    query = exchange(packed)
    near = lax.ppermute(kv[2 * GROUPS :], "plane", up)
    right = lax.ppermute(kv[:GROUPS], "plane", down)
    far = lax.ppermute(kv[GROUPS : 2 * GROUPS], "plane", up)

    def attend(frames, edges, place, earlier, slots_out, name, copied=True):
        blocks = BELOW + SLOTS + ABOVE
        units = len(frames)
        return pl.pallas_call(
            functools.partial(
                attend_kernel,
                frames,
                [span for span, _ in edges],
                [place] + [at for at, _ in earlier],
                copied,
                planes,
                256,
            ),
            out_shape=jax.ShapeDtypeStruct((slots_out * GROUPS, O_ROWS, HD), jnp.bfloat16),
            in_specs=[smem] + whole(3) + [HBM] * copied + whole(len(edges) - copied + len(earlier)),
            out_specs=HBM,
            scratch_shapes=[
                VMEM((blocks, ROWS * GROUPS, HD), jnp.bfloat16),
                VMEM((blocks, ROWS * GROUPS, 2 * HD), jnp.bfloat16),
                VMEM((blocks, PART * GROUPS, HD), jnp.bfloat16),
                VMEM((blocks, PART * GROUPS, 2 * HD), jnp.bfloat16),
                VMEM((units * GROUPS, O_ROWS, HD), jnp.bfloat16),
                pltpu.SemaphoreType.DMA((units,)),
                pltpu.SemaphoreType.DMA((2,)),
                pltpu.SemaphoreType.DMA((1,)),
            ]
            + [VMEM(edges[0][1].shape, jnp.bfloat16)] * copied,
            compiler_params=params(32),
            cost_estimate=pl.CostEstimate(
                flops=units * 500_000_000, bytes_accessed=4_000_000, transcendentals=units * 1_000_000
            ),
            name=name,
        )(offsets, kv, query, gate_table, *(x for _, x in edges), *(x for _, x in earlier))

    shifted = jnp.where(lax.axis_index("slot") == last, climbed, residual[0])
    moved = lax.ppermute(shifted, "slot", [(i, (i + 1) % SLOTS) for i in range(SLOTS)])
    upper = attend((0, 1, 2), [(BELOW + SLOTS, right), (1, near)], 0, [], 3, "attend_upper")
    upper, query = lax.optimization_barrier((upper, query))
    attended = attend((-1,), [(0, far), (1, near)], 0, [(1, upper)], SLOTS, "attend_lower")
    attended, moved = lax.optimization_barrier((attended, moved))
    parts = exchange(attended)
    updated = pl.pallas_call(
        combine_kernel,
        out_shape=jax.ShapeDtypeStruct(incoming.shape, jnp.bfloat16),
        in_specs=[pl.BlockSpec(memory_space=VMEM), HBM, pl.BlockSpec(memory_space=VMEM)],
        out_specs=HBM,
        scratch_shapes=[
            VMEM(incoming.shape, jnp.bfloat16),
            VMEM(incoming.shape, jnp.bfloat16),
            pltpu.SemaphoreType.DMA((GROUPS // 2,)),
            pltpu.SemaphoreType.DMA((GROUPS // 2,)),
        ],
        compiler_params=params(20),
        cost_estimate=pl.CostEstimate(flops=1_000, bytes_accessed=4_000_000, transcendentals=0),
        name="combine",
    )(parts, moved, incoming)
    return updated[None]


def solution(mesh):
    planes = mesh.shape["frame"] // SLOTS
    inner = Mesh(
        mesh.devices.reshape(planes, SLOTS, GROUPS), ("plane", "slot", "group")
    )
    frame = ("plane", "slot")
    tokens = P(frame, "group", None)
    placed = (
        tokens,
        tokens,
        tokens,
        tokens,
        P(),
        P(),
        P(None, "group"),
        P(frame),
        P(frame),
        P("group", None),
    )
    return jax.shard_map(
        functools.partial(on_device, planes), mesh=inner, in_specs=placed, out_specs=tokens, check_vma=False
    )
```
